256 devices in a mesh: rep: 32 (over x, y, core), section: 8 (over z).
Axes of the slice: x: 4, y: 4, z: 8, core: 2. Of those that a mesh axis runs over, the one named last changes fastest.
Arguments:
- inputs: bfloat16 [32, 4, 64, 5120], P('rep'), may hold values from -6 to 6
- cotangent: bfloat16 [32, 4, 64, 5120], P('rep'), may hold values from -6 to 6
- w_down: bfloat16 [8, 5120, 256], P('section'), may hold values from -0.078125 to 0.078125
- w_up: bfloat16 [8, 256, 5120], P('section'), may hold values from -0.375 to 0.375
- counts: int32 [32], replicated, may hold values from 0 to 4, as said below
Outputs:
- grad_down: float32 [8, 5120, 256], P('section', 'rep')
- grad_up: float32 [8, 256, 5120], P('section', 'rep')
- section_grads: bfloat16 [8, 32, 4, 64, 5120], P('section', 'rep')
The draws below stay inside these ranges and needn't reach their ends.
Inputs may be any that keep to these rules, and one draw needn't show every extreme that they name: Slots s < counts[p] of relay p hold live micro-batches, the others none; exactly one relay, the dropped one, has 0, and at least one has all 4.
All inputs are finite; a program needn't handle non-finite values.
Results may differ from the reference program's by a relative error of at most 0.033.
Values may be sent and summed in bfloat16 or wider, within the bound.
No kernel may reach another device: no remote copies, remote signals or barrier semaphores. Data moves between devices by JAX's collectives and lax.ppermute only.
A program may use at most 128 MiB of HBM per device.

```python
import jax
import jax.numpy as jnp
from jax import lax

D = 5120
R = 256
MB_TOK = 64
SLOTS = 4
PIPES = 32
LAYERS = 8


def draw_counts(key, part):
    key = jax.random.fold_in(key, 7)
    key_heavy, key_light, key_full, key_drop = jax.random.split(key, 4)
    heavy = jax.random.randint(key_heavy, (PIPES,), 0, 4) == 0
    light = jax.random.randint(key_light, (PIPES,), 1, 3)
    values = jnp.where(heavy, SLOTS, light)
    full_pipe = jax.random.randint(key_full, (), 0, PIPES)
    drop_pipe = (full_pipe + jax.random.randint(key_drop, (), 1, PIPES)) % PIPES
    places = jnp.arange(PIPES)
    values = jnp.where(places == full_pipe, SLOTS, values)
    values = jnp.where(places == drop_pipe, 0, values)
    return values.astype(jnp.int32)


def level_of(stream_key, shape, cuts, low, top_value):
    def one(axis_at, shards_of):
        steps = jax.random.uniform(jax.random.fold_in(jax.random.fold_in(stream_key, 6), axis_at), (shards_of,), jnp.float32, low / len(cuts), top_value / len(cuts))
        return jnp.repeat(jnp.exp(steps), shape[axis_at] // shards_of).reshape((-1,) + (1,) * (len(shape) - axis_at - 1))

    gain = one(*cuts[0])
    for cut in cuts[1:]:
        gain = gain * one(*cut)
    return gain


def normal_values(rng, extent, width, limit, pieces=(), held_as=jnp.bfloat16):
    values = jax.random.normal(rng, extent, jnp.float32) * width
    if len(pieces) > 0:
        values = level_of(rng, extent, pieces, -0.22, 0.18) * values
    return jnp.clip(values, min=-limit, max=limit).astype(held_as)


def setup_inputs(seed: int = 0) -> dict:
    streams_of = jax.random.split(jax.random.key(seed), 6)
    inputs = normal_values(streams_of[0], (PIPES, SLOTS, MB_TOK, D), 1.0, 6.0, ((0, 32),))
    cotangent = normal_values(streams_of[1], (PIPES, SLOTS, MB_TOK, D), 1.0, 6.0, ((0, 32),))
    w_down = normal_values(streams_of[2], (LAYERS, D, R), D ** -0.5, 0.078125, ((0, 8),))
    w_up = normal_values(streams_of[3], (LAYERS, R, D), R ** -0.5, 0.375, ((0, 8),))
    counts = draw_counts(jax.random.fold_in(streams_of[5], 71), 0)
    return dict(inputs=inputs, cotangent=cotangent, w_down=w_down, w_up=w_up, counts=counts)


def layer_forward(hidden, down_mat, up_mat):
    x_float = hidden.astype(jnp.float32)
    centered = x_float - lax.optimization_barrier(jnp.mean(x_float, axis=-1, keepdims=True))
    inv_std = lax.rsqrt(lax.optimization_barrier(jnp.mean(centered * centered, axis=-1, keepdims=True)) + 1e-05)
    normed = centered * inv_std
    normed_b = normed.astype(jnp.bfloat16)
    preact = jnp.dot(normed_b, down_mat, preferred_element_type=jnp.float32)
    act_b = jax.nn.gelu(preact, approximate=True).astype(jnp.bfloat16)
    output = (x_float + jnp.dot(act_b, up_mat, preferred_element_type=jnp.float32)).astype(jnp.bfloat16)
    return (output, normed, inv_std, preact, normed_b, act_b)

def layer_backward(incoming, normed, inv_std, preact, down_mat, up_mat):
    act_grad = lax.dot_general(incoming, up_mat, (((1,), (1,)), ((), ())), preferred_element_type=jnp.float32)
    pre_grad = jax.vjp(lambda value: jax.nn.gelu(value, approximate=True), preact)[1](act_grad)[0]
    pre_grad_b = pre_grad.astype(jnp.bfloat16)
    norm_grad = lax.dot_general(pre_grad_b, down_mat, (((1,), (1,)), ((), ())), preferred_element_type=jnp.float32)
    mean_one = lax.optimization_barrier(jnp.mean(norm_grad, axis=-1, keepdims=True))
    mean_two = lax.optimization_barrier(jnp.mean(norm_grad * normed, axis=-1, keepdims=True))
    back_float = incoming.astype(jnp.float32) + inv_std * (norm_grad - mean_one - normed * mean_two)
    return (back_float.astype(jnp.bfloat16), pre_grad_b)

def outer_sum(left, right):
    return lax.dot_general(left, right, (((0,), (0,)), ((), ())), preferred_element_type=jnp.float32)

def reference(inputs, cotangent, w_down, w_up, counts):
    entries = PIPES * SLOTS
    flat_in = inputs.reshape(entries, MB_TOK, D)
    flat_cot = cotangent.reshape(entries, MB_TOK, D)
    positions = jnp.arange(entries, dtype=jnp.int32)
    owners = positions // SLOTS
    slot_ids = positions % SLOTS
    is_live = (slot_ids < counts[owners]).astype(jnp.float32)

    def one_entry(state_pair, entry_data):
        grad_down, grad_up = state_pair
        x_entry, g_entry, alive = entry_data
        section_in = []
        hidden = x_entry
        for layer_idx in range(LAYERS):
            section_in.append(hidden)
            hidden = layer_forward(hidden, w_down[layer_idx], w_up[layer_idx])[0]
        incoming = g_entry
        results = [None] * LAYERS
        for layer_idx in reversed(range(LAYERS)):
            output, normed, inv_std, preact, normed_b, act_b = layer_forward(section_in[layer_idx], w_down[layer_idx], w_up[layer_idx])
            back_b, pre_grad_b = layer_backward(incoming, normed, inv_std, preact, w_down[layer_idx], w_up[layer_idx])
            grad_down = grad_down.at[layer_idx].add(alive * outer_sum(normed_b, pre_grad_b))
            grad_up = grad_up.at[layer_idx].add(alive * outer_sum(act_b, incoming))
            results[layer_idx] = jnp.where(alive > 0, back_b, jnp.zeros_like(back_b))
            incoming = back_b
        return ((grad_down, grad_up), jnp.stack(results))
    start_pair = (jnp.zeros((LAYERS, D, R), jnp.float32), jnp.zeros((LAYERS, R, D), jnp.float32))
    (grad_down, grad_up), stacked = lax.scan(one_entry, start_pair, (flat_in, flat_cot, is_live))
    grand_total = jnp.sum(counts).astype(jnp.float32)
    section_grads = stacked.reshape(PIPES, SLOTS, LAYERS, MB_TOK, D).transpose(2, 0, 1, 3, 4)
    return (grad_down / grand_total, grad_up / grand_total, section_grads)
```

```python
import functools

import jax
import jax.numpy as jnp
from jax import lax
from jax.experimental import pallas as pl
from jax.experimental.pallas import tpu as pltpu
from jax.sharding import PartitionSpec as P

F32 = jnp.float32
BF16 = jnp.bfloat16
CHUNK = 32
HOP = 2
TURNS = 10
VM = pltpu.VMEM


def gelu_pair(value):
    c = 0.7978845608028654
    square = value * value
    tan = jnp.tanh(c * (value + 0.044715 * value * square))
    act = 0.5 * value * (1.0 + tan)
    slope = 0.5 * (1.0 + tan) + 0.5 * value * (1.0 - tan * tan) * c * (1.0 + 0.134145 * square)
    return act, slope


def arriving(own, recv_ref, use_own):
    if recv_ref is None:
        return own
    return jnp.where(use_own, own, recv_ref[...].astype(F32))


def forward_part(row, own, first, ins, outs):
    hidden = arriving(own.astype(F32), ins.get("recv_f"), first)
    width = hidden.shape[1]
    centered = hidden - jnp.sum(hidden, axis=1, keepdims=True) * (1.0 / width)
    inv_std = lax.rsqrt(jnp.sum(centered * centered, axis=1, keepdims=True) * (1.0 / width) + 1e-05)
    normed_b = (centered * inv_std).astype(BF16)
    preact = jnp.dot(normed_b, ins["wd"][...], preferred_element_type=F32)
    act_b = gelu_pair(preact)[0].astype(BF16)
    outs["send_f"][...] = (
        hidden + jnp.dot(act_b, ins["wu"][...], preferred_element_type=F32)
    ).astype(BF16)
    rows = pl.ds(row, CHUNK)
    outs["nb"][rows, :] = normed_b
    outs["pre"][rows, :] = preact
    outs["act"][rows, :] = act_b
    outs["std"][rows, :] = jnp.broadcast_to(inv_std, (CHUNK, outs["std"].shape[1]))


def backward_part(row, at_row, own, last, live, ins, held, outs):
    incoming = arriving(own.astype(F32), ins.get("recv_b"), last)
    width = incoming.shape[1]
    act_grad = jnp.dot(incoming.astype(BF16), ins["wut"][...], preferred_element_type=F32)
    at_rows = pl.ds(at_row, CHUNK)
    preact = held["pre"][at_rows, :]
    pre_grad_b = (act_grad * gelu_pair(preact)[1]).astype(BF16)
    norm_grad = jnp.dot(pre_grad_b, ins["wdt"][...], preferred_element_type=F32)
    mean_one = jnp.sum(norm_grad, axis=1, keepdims=True) * (1.0 / width)
    mean_two = jnp.sum(pre_grad_b.astype(F32) * preact, axis=1, keepdims=True) * (1.0 / width)
    inv_std = jnp.max(held["std"][at_rows, :], axis=1, keepdims=True)
    normed = held["nb"][at_rows, :].astype(F32)
    back = incoming + inv_std * (norm_grad - mean_one - normed * mean_two)
    outs["send_b"][...] = back.astype(BF16)
    rows = pl.ds(row, CHUNK)
    outs["dy"][rows, :] = jnp.where(live, incoming, 0.0).astype(BF16)
    outs["grads"][rows, :] = jnp.where(live, back, 0.0).astype(BF16)
    outs["pg"][rows, :] = jnp.where(live, pre_grad_b.astype(F32), 0.0).astype(BF16)


def turn_part(turn, ins, outs):
    width = ins["wd"].shape[0]
    part = pl.ds(turn * (width // TURNS), width // TURNS)
    outs["wdt"][:, part] = ins["wd"][part, :].T
    outs["wut"][part, :] = ins["wu"][:, part].T


def step_kernel(plan, names_in, names_out, *all_refs):
    step, sections, tokens, slot_rows, do_forward, do_backward, turn = plan
    ins = dict(zip(names_in, all_refs[: len(names_in)]))
    outs = dict(zip(names_out, all_refs[len(names_in) :]))
    section, count = ins["info"][0], ins["info"][1]
    chunks = tokens // CHUNK

    def place(at):
        inside = (at >= 0) & (at < chunks)
        clipped = jnp.clip(at, 0, chunks - 1) * CHUNK
        row = pl.multiple_of(jnp.where(inside, clipped, tokens), CHUNK)
        return row, pl.multiple_of(clipped, CHUNK)

    if do_forward:
        row, _ = place(step - HOP * section)
        begin = min(step, chunks - 1) * CHUNK
        own = ins["x"][begin : begin + CHUNK, :]
        forward_part(row, own, section == 0, ins, outs)
    if do_backward:
        since = step - HOP * (sections - 1) - 1
        row, at_row = place(since - HOP * (sections - 1 - section))
        begin = min(since, chunks - 1) * CHUNK
        own = ins["g"][begin : begin + CHUNK, :]
        held = outs if do_forward else ins
        live = at_row // slot_rows < count
        backward_part(row, at_row, own, section == sections - 1, live, ins, held, outs)
    if turn is not None:
        turn_part(turn, ins, outs)


def run_step(plan, values, shapes):
    step, sections, tokens, slot_rows, do_forward, do_backward, turn = plan
    names_in = ["info"]
    names_out = []
    if do_forward:
        names_in += ["x", "recv_f", "wd", "wu"]
        names_out += ["send_f", "nb", "pre", "act", "std"]
    if do_backward:
        names_in += ["g", "recv_b", "wdt", "wut"]
        names_out += ["send_b", "dy", "grads", "pg"]
        if not do_forward:
            names_in += ["nb", "pre", "std"]
    if turn is not None:
        names_out += ["wdt", "wut"]
    names_in = [k for k in names_in if not (k.startswith("recv") and k not in values)]
    aliases = {}
    for at, name in enumerate(names_out):
        if name in values and not name.startswith("send"):
            aliases[len(names_in)] = at
            names_in.append(name)
    free = ("info", "recv_f", "recv_b")
    args = [
        values[k] if k in free else pltpu.with_memory_space_constraint(values[k], VM)
        for k in names_in
    ]
    out_shape = [
        jax.ShapeDtypeStruct(*shapes[k]) if k.startswith("send") else VM(*shapes[k])
        for k in names_out
    ]
    width, bottleneck = shapes["wdt"][0][::-1]
    results = pl.pallas_call(
        functools.partial(step_kernel, plan, names_in, names_out),
        out_shape=out_shape,
        in_specs=[
            pl.BlockSpec(memory_space=pltpu.SMEM if k == "info" else VM) for k in names_in
        ],
        out_specs=[pl.BlockSpec(memory_space=VM) for _ in names_out],
        input_output_aliases=aliases,
        cost_estimate=pl.CostEstimate(
            flops=4 * CHUNK * width * bottleneck * (do_forward + do_backward),
            bytes_accessed=4 * width * bottleneck,
            transcendentals=CHUNK * bottleneck,
        ),
        compiler_params=pltpu.CompilerParams(vmem_limit_bytes=8 * 1024 * 1024),
        name="step_" + ("f" if do_forward else "") + ("b" if do_backward else ""),
    )(*args)
    return dict(zip(names_out, results))


def outer(left, right):
    return lax.dot_general(left, right, (((0,), (0,)), ((), ())), preferred_element_type=F32)


def outer_kernel(tokens, reps, info, nb, act, dy, pg, mine, other, held):
    core = info[2]
    width, bottleneck = nb.shape[1], pg.shape[1]
    chips = reps // 2
    block = width // reps
    up_rows = bottleneck // reps
    each = mine.shape[0] // chips
    wide = 4 * block
    for at in range(width // wide):
        held[...] = outer(nb[:tokens, at * wide : (at + 1) * wide], pg[:tokens, :])
        for half in range(2):
            to = (2 * at + half) * each
            base = half * 2 * block
            mine[to : to + block, :] = held[pl.ds(base + core * block, block), :]
            other[to : to + block, :] = held[pl.ds(base + (1 - core) * block, block), :].astype(BF16)
    for at in range(width // bottleneck):
        held[:bottleneck, :] = outer(act[:tokens, :], dy[:tokens, at * bottleneck : (at + 1) * bottleneck])
        for chip in range(chips):
            base = chip * 2 * up_rows
            to = chip * each + block + at * up_rows
            mine[to : to + up_rows, :] = held[pl.ds(base + core * up_rows, up_rows), :]
            other[to : to + up_rows, :] = held[pl.ds(base + (1 - core) * up_rows, up_rows), :].astype(BF16)


def add_kernel(mine, came, total):
    total[...] = (mine[...] + came[...].astype(F32)).astype(BF16)


def final_kernel(scale, shares, down, up):
    chips, each, bottleneck = shares.shape
    block = down.shape[0]
    up_rows = up.shape[0]
    total = jnp.sum(shares[...].astype(F32), axis=0) / scale[0]
    down[...] = total[:block]
    for at in range(up.shape[1] // bottleneck):
        up[:, at * bottleneck : (at + 1) * bottleneck] = total[
            block + at * up_rows : block + (at + 1) * up_rows
        ]


def weight_grads(values, tokens, grand_total):
    reps = lax.axis_size("rep")
    chips = reps // 2
    width, bottleneck = values["wd"].shape
    block = width // reps
    up_rows = bottleneck // reps
    each = block + up_rows * (width // bottleneck)
    limit = pltpu.CompilerParams(vmem_limit_bytes=8 * 1024 * 1024)
    vmem = pl.BlockSpec(memory_space=VM)
    smem = pl.BlockSpec(memory_space=pltpu.SMEM)
    operands = [pltpu.with_memory_space_constraint(values[k], VM) for k in ("nb", "act", "dy", "pg")]
    mine, other = pl.pallas_call(
        functools.partial(outer_kernel, tokens, reps),
        out_shape=[VM((chips * each, bottleneck), F32), VM((chips * each, bottleneck), BF16)],
        in_specs=[smem] + [vmem] * 4,
        out_specs=[vmem, vmem],
        scratch_shapes=[VM((4 * block, bottleneck), F32)],
        compiler_params=limit,
        name="outer",
    )(values["info"], *operands)
    came = lax.ppermute(other, "rep", [(i, i ^ 1) for i in range(reps)])
    chip_sum = pl.pallas_call(
        add_kernel,
        out_shape=VM((chips * each, bottleneck), BF16),
        in_specs=[vmem, vmem],
        out_specs=vmem,
        compiler_params=limit,
        name="chip_sum",
    )(pltpu.with_memory_space_constraint(mine, VM), pltpu.with_memory_space_constraint(came, VM))
    groups = [[i for i in range(reps) if i % 2 == c] for c in (0, 1)]
    shares = lax.all_to_all(
        chip_sum.reshape(chips, each, bottleneck), "rep", 0, 0, axis_index_groups=groups
    )
    return pl.pallas_call(
        final_kernel,
        out_shape=[
            jax.ShapeDtypeStruct((block, bottleneck), F32),
            jax.ShapeDtypeStruct((up_rows, width), F32),
        ],
        in_specs=[smem, vmem],
        out_specs=[vmem, vmem],
        compiler_params=pltpu.CompilerParams(vmem_limit_bytes=16 * 1024 * 1024),
        name="final",
    )(grand_total[None], shares)


def body(inputs, cotangent, w_down, w_up, counts):
    sections = lax.axis_size("section")
    section = lax.axis_index("section")
    pipe = lax.axis_index("rep")
    slots, slot_rows, width = inputs.shape[1:]
    tokens = slots * slot_rows
    chunks = tokens // CHUNK
    bottleneck = w_down.shape[2]
    pipes = counts.shape[0]
    own_count = jnp.sum(jnp.where(jnp.arange(pipes) == pipe, counts, 0))
    grand_total = jnp.sum(counts).astype(F32)
    padded = tokens + CHUNK
    shapes = {
        "wdt": ((bottleneck, width), BF16),
        "wut": ((width, bottleneck), BF16),
        "send_f": ((CHUNK, width), BF16),
        "nb": ((padded, width), BF16),
        "pre": ((padded, bottleneck), F32),
        "act": ((padded, bottleneck), BF16),
        "std": ((padded, 128), F32),
        "send_b": ((CHUNK, width), BF16),
        "dy": ((padded, width), BF16),
        "grads": ((padded, width), BF16),
        "pg": ((padded, bottleneck), BF16),
    }
    values = {
        "info": jnp.stack([section, own_count, pipe % 2]).astype(jnp.int32),
        "x": inputs.reshape(tokens, width),
        "g": cotangent.reshape(tokens, width),
        "wd": w_down[0],
        "wu": w_up[0],
    }
    ahead = [(i, i + 1) for i in range(sections - 1)]
    behind = [(i + 1, i) for i in range(sections - 1)]
    start = HOP * (sections - 1) + 1
    forward_steps = chunks + HOP * (sections - 1)
    moved = {"f": {}, "b": {}}
    for step in range(start + forward_steps):
        do_forward = step < forward_steps
        do_backward = step >= start
        turn = step - 1 if 1 <= step <= TURNS else None
        for way in "fb":
            values.pop("recv_" + way, None)
            if step in moved[way]:
                values["recv_" + way] = moved[way].pop(step)
        plan = (step, sections, tokens, slot_rows, do_forward, do_backward, turn)
        results = run_step(plan, values, shapes)
        for way, ends, route in (
            ("f", forward_steps, ahead),
            ("b", start + forward_steps, behind),
        ):
            sent = results.pop("send_" + way, None)
            if sent is not None and step + HOP < ends:
                moved[way][step + HOP] = lax.ppermute(sent, "section", route)
        values.update(results)
    down_share, up_share = weight_grads(values, tokens, grand_total)
    grads_out = values["grads"][:tokens].reshape(1, 1, slots, slot_rows, width)
    return (down_share[None], up_share[None], grads_out)


def solution(mesh):
    in_specs = (
        P("rep", None, None, None),
        P("rep", None, None, None),
        P("section", None, None),
        P("section", None, None),
        P(),
    )
    out_specs = (
        P("section", "rep", None),
        P("section", "rep", None),
        P("section", "rep", None, None, None),
    )
    return jax.shard_map(body, mesh=mesh, in_specs=in_specs, out_specs=out_specs, check_vma=False)
```

```python
import functools

import jax
import jax.numpy as jnp
from jax import lax
from jax.experimental import pallas as pl
from jax.experimental.pallas import tpu as pltpu
from jax.sharding import PartitionSpec as P

F32 = jnp.float32
BF16 = jnp.bfloat16
CHUNK = 16
HOP = 2
TURNS = 10
PIECES = 4
COPIES = 8
VM = pltpu.VMEM


def gelu_pair(value):
    c = 0.7978845608028654
    square = value * value
    tan = jnp.tanh(c * (value + 0.044715 * value * square))
    act = 0.5 * value * (1.0 + tan)
    slope = 0.5 * (1.0 + tan) + 0.5 * value * (1.0 - tan * tan) * c * (1.0 + 0.134145 * square)
    return act, slope


def arriving(own, recv_ref, use_own):
    if recv_ref is None:
        return own
    return jnp.where(use_own, own, recv_ref[...].astype(F32))


def forward_part(row, own, first, ins, outs, weights):
    hidden = arriving(own.astype(F32), ins.get("recv_f"), first)
    width = hidden.shape[1]
    centered = hidden - jnp.sum(hidden, axis=1, keepdims=True) * (1.0 / width)
    inv_std = lax.rsqrt(jnp.sum(centered * centered, axis=1, keepdims=True) * (1.0 / width) + 1e-05)
    normed_b = (centered * inv_std).astype(BF16)
    preact = jnp.dot(normed_b, weights("wd"), preferred_element_type=F32)
    act_b = gelu_pair(preact)[0].astype(BF16)
    if "send_f" in outs:
        outs["send_f"][...] = (
            hidden + jnp.dot(act_b, weights("wu"), preferred_element_type=F32)
        ).astype(BF16)
    rows = pl.ds(row, CHUNK)
    outs["nb"][rows, :] = normed_b
    outs["pre"][rows, :] = preact
    outs["act"][rows, :] = act_b
    outs["std"][rows, :] = jnp.broadcast_to(inv_std, (CHUNK, outs["std"].shape[1]))


def backward_part(row, at_row, own, last, slot, ins, held, outs):
    incoming = arriving(own.astype(F32), ins.get("recv_b"), last)
    width = incoming.shape[1]
    at_rows = pl.ds(at_row, CHUNK)
    preact = held["pre"][at_rows, :]
    inv_std = jnp.max(held["std"][at_rows, :], axis=1, keepdims=True)
    normed = held["nb"][at_rows, :].astype(F32)
    live = jnp.where(ins["count"][:1, :1] > slot.astype(F32), 1.0, 0.0)
    act_grad = jnp.dot(incoming.astype(BF16), ins["wut"][...], preferred_element_type=F32)
    pre_grad = (act_grad * gelu_pair(preact)[1]).astype(BF16).astype(F32)
    mean_one = jnp.sum(pre_grad * ins["wmean"][:1, :], axis=1, keepdims=True)
    mean_two = jnp.sum(pre_grad * preact, axis=1, keepdims=True) * (1.0 / width)
    norm_grad = jnp.dot(pre_grad.astype(BF16), ins["wdt"][...], preferred_element_type=F32)
    back = incoming + inv_std * (norm_grad - mean_one - normed * mean_two)
    if "send_b" in outs:
        outs["send_b"][...] = back.astype(BF16)
    rows = pl.ds(row, CHUNK)
    outs["dy"][rows, :] = (incoming * live).astype(BF16)
    outs["grads"][rows, :] = (back * live).astype(BF16)
    outs["pg"][rows, :] = (pre_grad * live).astype(BF16)


def turn_part(turn, ins, outs):
    width = ins["wd"].shape[0]
    part = pl.ds(turn * (width // TURNS), width // TURNS)
    outs["wdt"][:, part] = ins["wd"][part, :].T
    outs["wut"][part, :] = ins["wu"][:, part].T


def mean_part(ins, outs):
    total = jnp.sum(ins["wd"][...].astype(F32), axis=0, keepdims=True)
    outs["wmean"][...] = jnp.broadcast_to(total * (1.0 / ins["wd"].shape[0]), outs["wmean"].shape)
    count = ins["counts"][lax.axis_index("rep")].astype(F32)
    outs["count"][...] = jnp.full(outs["count"].shape, count)


class Loader:
    def __init__(self, ins, outs, sems):
        self.outs = outs
        self.copies = {}
        for at, name in enumerate(("x", "wd", "wu")):
            source, target = ins["far_" + name], outs[name]
            size = source.shape[0] // PIECES
            self.copies[name] = [
                pltpu.make_async_copy(
                    source.at[part * size : (part + 1) * size],
                    target.at[part * size : (part + 1) * size],
                    sems.at[at, part],
                )
                for part in range(PIECES)
            ]
        order = [self.copies["x"][0], *self.copies["wd"], *self.copies["wu"], *self.copies["x"][1:]]
        for copy in order:
            copy.start()

    def wait(self, name, begin=0, end=None):
        for copy in self.copies[name][begin:end]:
            copy.wait()

    def __call__(self, name):
        self.wait(name)
        return self.outs[name][...]


def step_kernel(plan, names_in, names_out, *all_refs):
    step, sections, tokens, slot_rows, do_forward, do_backward, turn = plan
    ins = dict(zip(names_in, all_refs[: len(names_in)]))
    outs = dict(zip(names_out, all_refs[len(names_in) :]))
    section = lax.axis_index("section")
    chunks = tokens // CHUNK

    def place(at):
        inside = (at >= 0) & (at < chunks)
        clipped = jnp.clip(at, 0, chunks - 1) * CHUNK
        row = pl.multiple_of(jnp.where(inside, clipped, tokens), CHUNK)
        return row, pl.multiple_of(clipped, CHUNK)

    if do_backward:
        since = step - HOP * (sections - 1) - 1
        row, at_row = place(since - HOP * (sections - 1 - section))
        begin = min(since, chunks - 1) * CHUNK
        own = ins["g"][begin : begin + CHUNK, :]
        held = outs if do_forward else ins
        slot = at_row // slot_rows
        backward_part(row, at_row, own, section == sections - 1, slot, ins, held, outs)
    if do_forward:
        row, _ = place(step - HOP * section)
        begin = min(step, chunks - 1) * CHUNK
        if step == 0:
            load = Loader(ins, outs, all_refs[-1])
            load.wait("x", 0, 1)
            forward_part(row, outs["x"][:CHUNK, :], section == 0, ins, outs, load)
            load.wait("x", 1)
        else:
            own = ins["x"][begin : begin + CHUNK, :]
            forward_part(row, own, section == 0, ins, outs, lambda name: ins[name][...])
    if turn is not None and turn < TURNS:
        turn_part(turn, ins, outs)
    if turn == TURNS:
        mean_part(ins, outs)


def run_step(plan, values, shapes, sends):
    step, sections, tokens, slot_rows, do_forward, do_backward, turn = plan
    names_in = []
    names_out = []
    if do_forward:
        names_in += ["far_x", "far_wd", "far_wu"] if step == 0 else ["x", "recv_f", "wd", "wu"]
        names_out += ["x", "wd", "wu"] if step == 0 else []
        names_out += ["send_f", "nb", "pre", "act", "std"]
    if do_backward:
        names_in += ["g", "recv_b", "wdt", "wut", "wmean", "count"]
        names_out += ["send_b", "dy", "grads", "pg"]
        if not do_forward:
            names_in += ["nb", "pre", "std"]
    if turn is not None and turn < TURNS:
        names_out += ["wdt", "wut"]
    if turn == TURNS:
        names_in += ["counts"]
        names_out += ["wmean", "count"]
    names_in = [k for k in names_in if not (k.startswith("recv") and k not in values)]
    names_out = [k for k in names_out if k in sends or not k.startswith("send")]
    aliases = {}
    for at, name in enumerate(names_out):
        if name in values and not name.startswith("send"):
            aliases[len(names_in)] = at
            names_in.append(name)

    def placed(name):
        if name in ("counts", "recv_f", "recv_b"):
            return values[name]
        return pltpu.with_memory_space_constraint(
            values[name], pltpu.HBM if name.startswith("far") else VM
        )

    def spec(name):
        if name.startswith("far"):
            return pl.BlockSpec(memory_space=pltpu.HBM)
        return pl.BlockSpec(memory_space=pltpu.SMEM if name == "counts" else VM)

    out_shape = [
        jax.ShapeDtypeStruct(*shapes[k]) if k.startswith("send") else VM(*shapes[k])
        for k in names_out
    ]
    width, bottleneck = shapes["wd"][0]
    results = pl.pallas_call(
        functools.partial(step_kernel, plan, names_in, names_out),
        out_shape=out_shape,
        in_specs=[spec(k) for k in names_in],
        out_specs=[pl.BlockSpec(memory_space=VM) for _ in names_out],
        input_output_aliases=aliases,
        scratch_shapes=[pltpu.SemaphoreType.DMA((3, PIECES))] if step == 0 else [],
        cost_estimate=pl.CostEstimate(
            flops=4 * CHUNK * width * bottleneck * (do_forward + do_backward),
            bytes_accessed=4 * width * bottleneck,
            transcendentals=CHUNK * bottleneck,
        ),
        compiler_params=pltpu.CompilerParams(vmem_limit_bytes=8 * 1024 * 1024),
        name="step_" + ("f" if do_forward else "") + ("b" if do_backward else ""),
    )(*[placed(k) for k in names_in])
    return dict(zip(names_out, results))


def outer(left, right):
    return lax.dot_general(left, right, (((0,), (0,)), ((), ())), preferred_element_type=F32)


def outer_kernel(tokens, reps, nb, act, dy, pg, grads, mine, other, grads_out, held, sem):
    core = lax.rem(lax.axis_index("rep"), 2)
    size = tokens // COPIES
    copies = [
        pltpu.make_async_copy(
            grads.at[at * size : (at + 1) * size],
            grads_out.at[at * size : (at + 1) * size],
            sem.at[at],
        )
        for at in range(COPIES)
    ]
    for copy in copies:
        copy.start()
    width, bottleneck = nb.shape[1], pg.shape[1]
    chips = reps // 2
    block = width // reps
    up_rows = bottleneck // reps
    each = mine.shape[0] // chips
    wide = 4 * block
    for at in range(width // wide):
        held[...] = outer(nb[:tokens, at * wide : (at + 1) * wide], pg[:tokens, :])
        for half in range(2):
            to = (2 * at + half) * each
            base = half * 2 * block
            mine[to : to + block, :] = held[pl.ds(base + core * block, block), :]
            other[to : to + block, :] = held[pl.ds(base + (1 - core) * block, block), :].astype(BF16)
    for at in range(width // bottleneck):
        held[:bottleneck, :] = outer(act[:tokens, :], dy[:tokens, at * bottleneck : (at + 1) * bottleneck])
        for chip in range(chips):
            base = chip * 2 * up_rows
            to = chip * each + block + at * up_rows
            mine[to : to + up_rows, :] = held[pl.ds(base + core * up_rows, up_rows), :]
            other[to : to + up_rows, :] = held[pl.ds(base + (1 - core) * up_rows, up_rows), :].astype(BF16)
    for copy in copies:
        copy.wait()


def add_kernel(mine, came, total):
    total[...] = (mine[...] + came[...].astype(F32)).astype(BF16)


def final_kernel(counts, shares, down, up):
    chips, each, bottleneck = shares.shape
    block = down.shape[0]
    up_rows = up.shape[0]
    live = counts[0]
    for at in range(1, counts.shape[0]):
        live = live + counts[at]
    total = jnp.sum(shares[...].astype(F32), axis=0) / live.astype(F32)
    down[...] = total[:block]
    for at in range(up.shape[1] // bottleneck):
        up[:, at * bottleneck : (at + 1) * bottleneck] = total[
            block + at * up_rows : block + (at + 1) * up_rows
        ]


def weight_grads(values, tokens):
    reps = lax.axis_size("rep")
    chips = reps // 2
    width, bottleneck = values["wd"].shape
    block = width // reps
    up_rows = bottleneck // reps
    each = block + up_rows * (width // bottleneck)
    limit = pltpu.CompilerParams(vmem_limit_bytes=8 * 1024 * 1024)
    vmem = pl.BlockSpec(memory_space=VM)
    smem = pl.BlockSpec(memory_space=pltpu.SMEM)
    operands = [pltpu.with_memory_space_constraint(values[k], VM) for k in ("nb", "act", "dy", "pg", "grads")]
    mine, other, grads_out = pl.pallas_call(
        functools.partial(outer_kernel, tokens, reps),
        out_shape=[
            VM((chips * each, bottleneck), F32),
            VM((chips * each, bottleneck), BF16),
            pltpu.HBM((tokens, width), BF16),
        ],
        in_specs=[vmem] * 5,
        out_specs=[vmem, vmem, pl.BlockSpec(memory_space=pltpu.HBM)],
        scratch_shapes=[VM((4 * block, bottleneck), F32), pltpu.SemaphoreType.DMA((COPIES,))],
        compiler_params=limit,
        name="outer",
    )(*operands)
    came = lax.ppermute(other, "rep", [(i, i ^ 1) for i in range(reps)])
    chip_sum = pl.pallas_call(
        add_kernel,
        out_shape=VM((chips * each, bottleneck), BF16),
        in_specs=[vmem, vmem],
        out_specs=vmem,
        compiler_params=limit,
        name="chip_sum",
    )(pltpu.with_memory_space_constraint(mine, VM), pltpu.with_memory_space_constraint(came, VM))
    groups = [[i for i in range(reps) if i % 2 == c] for c in (0, 1)]
    shares = lax.all_to_all(
        chip_sum.reshape(chips, each, bottleneck), "rep", 0, 0, axis_index_groups=groups
    )
    down, up = pl.pallas_call(
        final_kernel,
        out_shape=[
            jax.ShapeDtypeStruct((block, bottleneck), F32),
            jax.ShapeDtypeStruct((up_rows, width), F32),
        ],
        in_specs=[smem, vmem],
        out_specs=[vmem, vmem],
        compiler_params=pltpu.CompilerParams(vmem_limit_bytes=16 * 1024 * 1024),
        name="final",
    )(values["counts"], shares)
    return down, up, grads_out


def body(inputs, cotangent, w_down, w_up, counts):
    sections = lax.axis_size("section")
    slots, slot_rows, width = inputs.shape[1:]
    tokens = slots * slot_rows
    chunks = tokens // CHUNK
    bottleneck = w_down.shape[2]
    padded = tokens + CHUNK
    shapes = {
        "x": ((tokens, width), BF16),
        "wd": ((width, bottleneck), BF16),
        "wu": ((bottleneck, width), BF16),
        "wmean": ((8, bottleneck), F32),
        "count": ((8, 128), F32),
        "wdt": ((bottleneck, width), BF16),
        "wut": ((width, bottleneck), BF16),
        "send_f": ((CHUNK, width), BF16),
        "nb": ((padded, width), BF16),
        "pre": ((padded, bottleneck), F32),
        "act": ((padded, bottleneck), BF16),
        "std": ((padded, 128), F32),
        "send_b": ((CHUNK, width), BF16),
        "dy": ((padded, width), BF16),
        "grads": ((padded, width), BF16),
        "pg": ((padded, bottleneck), BF16),
    }
    values = {
        "counts": counts,
        "far_x": inputs.reshape(tokens, width),
        "far_wd": w_down[0],
        "far_wu": w_up[0],
        "g": cotangent.reshape(tokens, width),
    }
    ahead = [(i, (i + 1) % sections) for i in range(sections)]
    behind = [(b, a) for a, b in ahead]
    start = HOP * (sections - 1) + 1
    forward_steps = chunks + HOP * (sections - 1)
    ends = {"send_f": forward_steps, "send_b": start + forward_steps}
    moved = {"f": {}, "b": {}}
    for step in range(start + forward_steps):
        do_forward = step < forward_steps
        do_backward = step >= start
        turn = step - 1 if 1 <= step <= TURNS + 1 else None
        for way in "fb":
            values.pop("recv_" + way, None)
            if step in moved[way]:
                values["recv_" + way] = moved[way].pop(step)
        plan = (step, sections, tokens, slot_rows, do_forward, do_backward, turn)
        sends = [k for k, end in ends.items() if step + HOP < end]
        results = run_step(plan, values, shapes, sends)
        for way, route in (("f", ahead), ("b", behind)):
            if "send_" + way in results:
                sent = results.pop("send_" + way)
                moved[way][step + HOP] = lax.ppermute(sent, "section", route)
        values.update(results)
    down_share, up_share, grads_out = weight_grads(values, tokens)
    return (
        down_share[None],
        up_share[None],
        grads_out.reshape(1, 1, slots, slot_rows, width),
    )


def solution(mesh):
    in_specs = (
        P("rep", None, None, None),
        P("rep", None, None, None),
        P("section", None, None),
        P("section", None, None),
        P(),
    )
    out_specs = (
        P("section", "rep", None),
        P("section", "rep", None),
        P("section", "rep", None, None, None),
    )
    return jax.shard_map(body, mesh=mesh, in_specs=in_specs, out_specs=out_specs, check_vma=False)
```

```python
import functools

import jax
import jax.numpy as jnp
from jax import lax
from jax.experimental import pallas as pl
from jax.experimental.pallas import tpu as pltpu
from jax.sharding import PartitionSpec as P

F32 = jnp.float32
BF16 = jnp.bfloat16
CHUNK = 16
HOP = 2
TURNS = 10
PIECES = 4
COPIES = 8
DEALT = (0, 2, 1, 3)
VM = pltpu.VMEM


def gelu_pair(value):
    c = 0.7978845608028654
    square = value * value
    tan = jnp.tanh(c * (value + 0.044715 * value * square))
    act = 0.5 * value * (1.0 + tan)
    slope = 0.5 * (1.0 + tan) + 0.5 * value * (1.0 - tan * tan) * c * (1.0 + 0.134145 * square)
    return act, slope


def arriving(own, recv_ref, use_own):
    if recv_ref is None:
        return own
    return jnp.where(use_own, own, recv_ref[...].astype(F32))


def forward_part(row, own, first, ins, outs, weights):
    hidden = arriving(own.astype(F32), ins.get("recv_f"), first)
    width = hidden.shape[1]
    centered = hidden - jnp.sum(hidden, axis=1, keepdims=True) * (1.0 / width)
    inv_std = lax.rsqrt(jnp.sum(centered * centered, axis=1, keepdims=True) * (1.0 / width) + 1e-05)
    normed_b = (centered * inv_std).astype(BF16)
    preact = jnp.dot(normed_b, weights("wd"), preferred_element_type=F32)
    act_b = gelu_pair(preact)[0].astype(BF16)
    if "send_f" in outs:
        outs["send_f"][...] = (
            hidden + jnp.dot(act_b, weights("wu"), preferred_element_type=F32)
        ).astype(BF16)
    rows = pl.ds(row, CHUNK)
    outs["nb"][rows, :] = normed_b
    outs["pre"][rows, :] = preact
    outs["act"][rows, :] = act_b
    outs["std"][rows, :] = jnp.broadcast_to(inv_std, (CHUNK, outs["std"].shape[1]))


def backward_part(row, at_row, own, last, slot, ins, held, outs):
    incoming = arriving(own.astype(F32), ins.get("recv_b"), last)
    width = incoming.shape[1]
    at_rows = pl.ds(at_row, CHUNK)
    preact = held["pre"][at_rows, :]
    inv_std = jnp.max(held["std"][at_rows, :], axis=1, keepdims=True)
    normed = held["nb"][at_rows, :].astype(F32)
    live = jnp.where(ins["count"][:1, :1] > slot.astype(F32), 1.0, 0.0)
    act_grad = jnp.dot(incoming.astype(BF16), ins["wut"][...], preferred_element_type=F32)
    pre_grad = (act_grad * gelu_pair(preact)[1]).astype(BF16).astype(F32)
    mean_one = jnp.sum(pre_grad * ins["wmean"][:1, :], axis=1, keepdims=True)
    mean_two = jnp.sum(pre_grad * preact, axis=1, keepdims=True) * (1.0 / width)
    norm_grad = jnp.dot(pre_grad.astype(BF16), ins["wdt"][...], preferred_element_type=F32)
    back = incoming + inv_std * (norm_grad - mean_one - normed * mean_two)
    if "send_b" in outs:
        outs["send_b"][...] = back.astype(BF16)
    rows = pl.ds(row, CHUNK)
    outs["dy"][rows, :] = (incoming * live).astype(BF16)
    outs["grads"][rows, :] = (back * live).astype(BF16)
    outs["pg"][rows, :] = (pre_grad * live).astype(BF16)


def turn_part(turn, ins, outs):
    width = ins["wd"].shape[0]
    part = pl.ds(turn * (width // TURNS), width // TURNS)
    outs["wdt"][:, part] = ins["wd"][part, :].T
    outs["wut"][part, :] = ins["wu"][:, part].T


def mean_part(ins, outs):
    total = jnp.sum(ins["wd"][...].astype(F32), axis=0, keepdims=True)
    outs["wmean"][...] = jnp.broadcast_to(total * (1.0 / ins["wd"].shape[0]), outs["wmean"].shape)
    count = ins["counts"][lax.axis_index("rep")].astype(F32)
    outs["count"][...] = jnp.full(outs["count"].shape, count)


class Loader:
    def __init__(self, ins, outs, sems):
        self.outs = outs
        self.copies = {}
        for at, name in enumerate(("x", "wd", "wu")):
            source, target = ins["far_" + name], outs[name]
            size = source.shape[0] // PIECES
            self.copies[name] = [
                pltpu.make_async_copy(
                    source.at[part * size : (part + 1) * size],
                    target.at[part * size : (part + 1) * size],
                    sems.at[at, part],
                )
                for part in range(PIECES)
            ]
        order = [self.copies["x"][0], *self.copies["wd"], *self.copies["wu"], *self.copies["x"][1:]]
        for copy in order:
            copy.start()

    def wait(self, name, begin=0, end=None):
        for copy in self.copies[name][begin:end]:
            copy.wait()

    def __call__(self, name):
        self.wait(name)
        return self.outs[name][...]


def step_kernel(plan, names_in, names_out, *all_refs):
    step, sections, tokens, slot_rows, do_forward, do_backward, turn = plan
    ins = dict(zip(names_in, all_refs[: len(names_in)]))
    outs = dict(zip(names_out, all_refs[len(names_in) :]))
    section = lax.axis_index("section")
    chunks = tokens // CHUNK

    def place(at):
        inside = (at >= 0) & (at < chunks)
        clipped = jnp.clip(at, 0, chunks - 1) * CHUNK
        row = pl.multiple_of(jnp.where(inside, clipped, tokens), CHUNK)
        return row, pl.multiple_of(clipped, CHUNK)

    if do_backward:
        since = step - HOP * (sections - 1) - 1
        row, at_row = place(since - HOP * (sections - 1 - section))
        begin = min(since, chunks - 1) * CHUNK
        own = ins["g"][begin : begin + CHUNK, :]
        held = outs if do_forward else ins
        slot = at_row // slot_rows
        backward_part(row, at_row, own, section == sections - 1, slot, ins, held, outs)
    if do_forward:
        row, _ = place(step - HOP * section)
        begin = min(step, chunks - 1) * CHUNK
        if step == 0:
            load = Loader(ins, outs, all_refs[-1])
            load.wait("x", 0, 1)
            forward_part(row, outs["x"][:CHUNK, :], section == 0, ins, outs, load)
            load.wait("x", 1)
        else:
            own = ins["x"][begin : begin + CHUNK, :]
            forward_part(row, own, section == 0, ins, outs, lambda name: ins[name][...])
    if turn is not None and turn < TURNS:
        turn_part(turn, ins, outs)
    if turn == TURNS:
        mean_part(ins, outs)


def run_step(plan, values, shapes, sends):
    step, sections, tokens, slot_rows, do_forward, do_backward, turn = plan
    names_in = []
    names_out = []
    if do_forward:
        names_in += ["far_x", "far_wd", "far_wu"] if step == 0 else ["x", "recv_f", "wd", "wu"]
        names_out += ["x", "wd", "wu"] if step == 0 else []
        names_out += ["send_f", "nb", "pre", "act", "std"]
    if do_backward:
        names_in += ["g", "recv_b", "wdt", "wut", "wmean", "count"]
        names_out += ["send_b", "dy", "grads", "pg"]
        if not do_forward:
            names_in += ["nb", "pre", "std"]
    if turn is not None and turn < TURNS:
        names_out += ["wdt", "wut"]
    if turn == TURNS:
        names_in += ["counts"]
        names_out += ["wmean", "count"]
    names_in = [k for k in names_in if not (k.startswith("recv") and k not in values)]
    names_out = [k for k in names_out if k in sends or not k.startswith("send")]
    aliases = {}
    for at, name in enumerate(names_out):
        if name in values and not name.startswith("send"):
            aliases[len(names_in)] = at
            names_in.append(name)

    def placed(name):
        if name in ("counts", "recv_f", "recv_b"):
            return values[name]
        return pltpu.with_memory_space_constraint(
            values[name], pltpu.HBM if name.startswith("far") else VM
        )

    def spec(name):
        if name.startswith("far"):
            return pl.BlockSpec(memory_space=pltpu.HBM)
        return pl.BlockSpec(memory_space=pltpu.SMEM if name == "counts" else VM)

    out_shape = [
        jax.ShapeDtypeStruct(*shapes[k]) if k.startswith("send") else VM(*shapes[k])
        for k in names_out
    ]
    width, bottleneck = shapes["wd"][0]
    results = pl.pallas_call(
        functools.partial(step_kernel, plan, names_in, names_out),
        out_shape=out_shape,
        in_specs=[spec(k) for k in names_in],
        out_specs=[pl.BlockSpec(memory_space=VM) for _ in names_out],
        input_output_aliases=aliases,
        scratch_shapes=[pltpu.SemaphoreType.DMA((3, PIECES))] if step == 0 else [],
        cost_estimate=pl.CostEstimate(
            flops=4 * CHUNK * width * bottleneck * (do_forward + do_backward),
            bytes_accessed=4 * width * bottleneck,
            transcendentals=CHUNK * bottleneck,
        ),
        compiler_params=pltpu.CompilerParams(vmem_limit_bytes=8 * 1024 * 1024),
        name="step_" + ("f" if do_forward else "") + ("b" if do_backward else ""),
    )(*[placed(k) for k in names_in])
    return dict(zip(names_out, results))


def outer(left, right):
    return lax.dot_general(left, right, (((0,), (0,)), ((), ())), preferred_element_type=F32)


def outer_down_kernel(tokens, reps, nb, pg, mine, other, held):
    core = lax.rem(lax.axis_index("rep"), 2)
    width = nb.shape[1]
    block = width // reps
    wide = 4 * block
    for at in range(width // wide):
        held[...] = outer(nb[:tokens, at * wide : (at + 1) * wide], pg[:tokens, :])
        for half in range(2):
            to = (2 * at + half) * block
            base = half * 2 * block
            mine[to : to + block, :] = held[pl.ds(base + core * block, block), :]
            other[to : to + block, :] = held[pl.ds(base + (1 - core) * block, block), :].astype(BF16)


def outer_up_kernel(tokens, reps, act, dy, mine, other, held, wide):
    core = lax.rem(lax.axis_index("rep"), 2)
    bottleneck, width = act.shape[1], dy.shape[1]
    chips = reps // 2
    rows = bottleneck // reps
    each = rows * (width // bottleneck)
    for at in range(width // bottleneck):
        held[...] = outer(act[:tokens, :], dy[:tokens, at * bottleneck : (at + 1) * bottleneck])
        for chip in range(chips):
            base = chip * 2 * rows
            to = chip * each + at * rows
            mine[to : to + rows, :] = held[pl.ds(base + core * rows, rows), :]
            wide[to : to + rows, :] = held[pl.ds(base + (1 - core) * rows, rows), :]
    other[...] = wide[...].astype(BF16)


def place_in(axis_first, side):
    chip = lax.axis_index("rep") // 2
    return chip // side if axis_first == "x" else lax.rem(chip, side)


def chip_sum_kernel(axis, side, mine, came, keep, *sends):
    me = place_in(axis, side)
    each = mine.shape[0] // (side * side)
    step, other = (side, 1) if axis == "x" else (1, side)
    for ahead, out in zip(DEALT, (keep, *sends)):
        to = lax.rem(me + ahead, side)
        for at in range(side):
            chip = to * step + at * other
            rows = pl.ds(pl.multiple_of(chip * each, each), each)
            part = mine[rows, :] + came[rows, :].astype(F32)
            out[at * each : (at + 1) * each, :] = part.astype(out.dtype)


def axis_sum_kernel(axis, side, keep, *refs):
    came, outs = refs[: side - 1], refs[side:]
    me = place_in("y" if axis == "x" else "x", side)
    each = keep.shape[0] // side
    for ahead, out in zip(DEALT, outs):
        to = lax.rem(me + ahead, side)
        rows = pl.ds(pl.multiple_of(to * each, each), each)
        total = keep[rows, :]
        for ref in came:
            total = total + ref[rows, :].astype(F32)
        out[...] = total.astype(out.dtype)


def final_kernel(side, counts, *refs):
    live = counts[0]
    for at in range(1, counts.shape[0]):
        live = live + counts[at]
    scale = live.astype(F32)
    for which, out in enumerate(refs[2 * side :]):
        total = refs[which * side][...]
        for ref in refs[which * side + 1 : (which + 1) * side]:
            total = total + ref[...].astype(F32)
        total = total / scale
        rows, bottleneck = out.shape[0], total.shape[1]
        for at in range(out.shape[1] // bottleneck):
            out[:, at * bottleneck : (at + 1) * bottleneck] = total[at * rows : (at + 1) * rows]


def store_kernel(tokens, grads, after, out, sems):
    size = tokens // COPIES
    copies = [
        pltpu.make_async_copy(
            grads.at[at * size : (at + 1) * size], out.at[at * size : (at + 1) * size], sems.at[at]
        )
        for at in range(COPIES)
    ]
    for copy in copies:
        copy.start()
    for copy in copies:
        copy.wait()


def call(kernel, name, out_shape, args, scratch=(), specs=None, out_specs=None):
    vmem = pl.BlockSpec(memory_space=VM)
    several = isinstance(out_shape, list)
    return pl.pallas_call(
        kernel,
        out_shape=out_shape,
        in_specs=specs or [vmem] * len(args),
        out_specs=out_specs or ([vmem] * len(out_shape) if several else vmem),
        scratch_shapes=list(scratch),
        compiler_params=pltpu.CompilerParams(vmem_limit_bytes=12 * 1024 * 1024),
        name=name,
    )(*args)


def weight_grads(values, tokens):
    reps = lax.axis_size("rep")
    chips = reps // 2
    side = round(chips**0.5)
    nb, act, dy, pg, grads = (
        pltpu.with_memory_space_constraint(values[k], VM) for k in ("nb", "act", "dy", "pg", "grads")
    )
    width, bottleneck = nb.shape[1], pg.shape[1]
    block = width // reps
    each = {"down": block, "up": (bottleneck // reps) * (width // bottleneck)}
    partner = [(i, i ^ 1) for i in range(reps)]

    def route(axis, ahead):
        def target(i):
            x, y, core = i // 2 // side, i // 2 % side, i % 2
            if axis == "x":
                x = (x + ahead) % side
            else:
                y = (y + ahead) % side
            return (x * side + y) * 2 + core

        return [(i, target(i)) for i in range(reps)]

    def outers(name, kernel, args, scratch):
        rows = chips * each[name]
        shapes = [VM((rows, bottleneck), F32), VM((rows, bottleneck), BF16)]
        mine, other = call(
            functools.partial(kernel, tokens, reps), "outer_" + name, shapes, args, scratch
        )
        return mine, lax.ppermute(other, "rep", partner)

    def parts(rows):
        sends = [jax.ShapeDtypeStruct((rows, bottleneck), BF16) for _ in range(side - 1)]
        return [VM((rows, bottleneck), F32), *sends]

    halves = {
        "down": outers("down", outer_down_kernel, (nb, pg), [VM((4 * block, bottleneck), F32)]),
        "up": outers(
            "up",
            outer_up_kernel,
            (act, dy),
            [VM((bottleneck, bottleneck), F32), VM((chips * each["up"], bottleneck), F32)],
        ),
    }
    first = {"down": "x", "up": "y"}
    second = {"down": "y", "up": "x"}
    sums, shares = {}, {}
    for name, (mine, came) in halves.items():
        mine = pltpu.with_memory_space_constraint(mine, VM)
        kernel = functools.partial(chip_sum_kernel, first[name], side)
        keep, *sends = call(kernel, "chip_sum_" + name, parts(side * each[name]), (mine, came))
        after = sends[-1]
        came = [lax.ppermute(s, "rep", route(first[name], k)) for k, s in zip(DEALT[1:], sends)]
        sums[name] = (keep, *came)
    any_spec = pl.BlockSpec(memory_space=pl.ANY)
    far_spec = pl.BlockSpec(memory_space=pltpu.HBM)
    grads_out = call(
        functools.partial(store_kernel, tokens),
        "store",
        pltpu.HBM((tokens, width), BF16),
        (grads, after),
        [pltpu.SemaphoreType.DMA((COPIES,))],
        [pl.BlockSpec(memory_space=VM), any_spec],
        far_spec,
    )
    stored = pltpu.with_memory_space_constraint(grads_out, pltpu.HBM)
    for name, (keep, *came) in sums.items():
        keep = pltpu.with_memory_space_constraint(keep, VM)
        kernel = functools.partial(axis_sum_kernel, first[name], side)
        args, specs = [keep, *came], [pl.BlockSpec(memory_space=VM)] * side
        keep, *sends = call(
            kernel, "axis_sum_" + name, parts(each[name]), [*args, stored], specs=[*specs, far_spec]
        )
        came = [lax.ppermute(s, "rep", route(second[name], k)) for k, s in zip(DEALT[1:], sends)]
        shares[name] = (keep, *came)
    args = [values["counts"]]
    for keep, *came in shares.values():
        args += [pltpu.with_memory_space_constraint(keep, VM), *came]
    shapes = [(block, bottleneck), (bottleneck // reps, width)]
    down, up = call(
        functools.partial(final_kernel, side),
        "final",
        [jax.ShapeDtypeStruct(shape, F32) for shape in shapes],
        args,
        specs=[pl.BlockSpec(memory_space=pltpu.SMEM)]
        + [pl.BlockSpec(memory_space=VM)] * (len(args) - 1),
    )
    return down, up, grads_out


def body(inputs, cotangent, w_down, w_up, counts):
    sections = lax.axis_size("section")
    slots, slot_rows, width = inputs.shape[1:]
    tokens = slots * slot_rows
    chunks = tokens // CHUNK
    bottleneck = w_down.shape[2]
    padded = tokens + CHUNK
    shapes = {
        "x": ((tokens, width), BF16),
        "wd": ((width, bottleneck), BF16),
        "wu": ((bottleneck, width), BF16),
        "wmean": ((8, bottleneck), F32),
        "count": ((8, 128), F32),
        "wdt": ((bottleneck, width), BF16),
        "wut": ((width, bottleneck), BF16),
        "send_f": ((CHUNK, width), BF16),
        "nb": ((padded, width), BF16),
        "pre": ((padded, bottleneck), F32),
        "act": ((padded, bottleneck), BF16),
        "std": ((padded, 128), F32),
        "send_b": ((CHUNK, width), BF16),
        "dy": ((padded, width), BF16),
        "grads": ((padded, width), BF16),
        "pg": ((padded, bottleneck), BF16),
    }
    values = {
        "counts": counts,
        "far_x": inputs.reshape(tokens, width),
        "far_wd": w_down[0],
        "far_wu": w_up[0],
        "g": cotangent.reshape(tokens, width),
    }
    ahead = [(i, (i + 1) % sections) for i in range(sections)]
    behind = [(b, a) for a, b in ahead]
    start = HOP * (sections - 1) + 1
    forward_steps = chunks + HOP * (sections - 1)
    ends = {"send_f": forward_steps, "send_b": start + forward_steps}
    moved = {"f": {}, "b": {}}
    for step in range(start + forward_steps):
        do_forward = step < forward_steps
        do_backward = step >= start
        turn = step - 1 if 1 <= step <= TURNS + 1 else None
        for way in "fb":
            values.pop("recv_" + way, None)
            if step in moved[way]:
                values["recv_" + way] = moved[way].pop(step)
        plan = (step, sections, tokens, slot_rows, do_forward, do_backward, turn)
        sends = [k for k, end in ends.items() if step + HOP < end]
        results = run_step(plan, values, shapes, sends)
        for way, route in (("f", ahead), ("b", behind)):
            if "send_" + way in results:
                sent = results.pop("send_" + way)
                moved[way][step + HOP] = lax.ppermute(sent, "section", route)
        values.update(results)
    down_share, up_share, grads_out = weight_grads(values, tokens)
    return (
        down_share[None],
        up_share[None],
        grads_out.reshape(1, 1, slots, slot_rows, width),
    )


def solution(mesh):
    in_specs = (
        P("rep", None, None, None),
        P("rep", None, None, None),
        P("section", None, None),
        P("section", None, None),
        P(),
    )
    out_specs = (
        P("section", "rep", None),
        P("section", "rep", None),
        P("section", "rep", None, None, None),
    )
    return jax.shard_map(body, mesh=mesh, in_specs=in_specs, out_specs=out_specs, check_vma=False)
```

```python
import functools

import jax
import jax.numpy as jnp
from jax import lax
from jax.experimental import pallas as pl
from jax.experimental.pallas import tpu as pltpu
from jax.sharding import PartitionSpec as P

F32 = jnp.float32
BF16 = jnp.bfloat16
CHUNK = 16
HOP = 2
TURNS = 10
PIECES = 4
COPIES = 8
DEALT = (0, 2, 1, 3)
VM = pltpu.VMEM


def gelu_pair(value):
    c = 0.7978845608028654
    square = value * value
    tan = jnp.tanh(c * (value + 0.044715 * value * square))
    act = 0.5 * value * (1.0 + tan)
    slope = 0.5 * (1.0 + tan) + 0.5 * value * (1.0 - tan * tan) * c * (1.0 + 0.134145 * square)
    return act, slope


def arriving(own, recv_ref, use_own):
    if recv_ref is None:
        return own
    return jnp.where(use_own, own, recv_ref[...].astype(F32))


def forward_part(row, own, first, ins, outs, weights):
    hidden = arriving(own.astype(F32), ins.get("recv_f"), first)
    width = hidden.shape[1]
    centered = hidden - jnp.sum(hidden, axis=1, keepdims=True) * (1.0 / width)
    inv_std = lax.rsqrt(jnp.sum(centered * centered, axis=1, keepdims=True) * (1.0 / width) + 1e-05)
    preact = jnp.dot(centered.astype(BF16), weights("wd"), preferred_element_type=F32) * inv_std
    act_b = gelu_pair(preact)[0].astype(BF16)
    if "send_f" in outs:
        outs["send_f"][...] = (
            hidden + jnp.dot(act_b, weights("wu"), preferred_element_type=F32)
        ).astype(BF16)
    rows = pl.ds(row, CHUNK)
    outs["nb"][rows, :] = (centered * inv_std).astype(BF16)
    outs["pre"][rows, :] = preact
    outs["act"][rows, :] = act_b
    outs["std"][rows, :] = jnp.broadcast_to(inv_std, (CHUNK, outs["std"].shape[1]))


def backward_part(row, at_row, own, last, slot, ins, held, outs):
    incoming = arriving(own.astype(F32), ins.get("recv_b"), last)
    width = incoming.shape[1]
    at_rows = pl.ds(at_row, CHUNK)
    preact = held["pre"][at_rows, :]
    inv_std = jnp.max(held["std"][at_rows, :], axis=1, keepdims=True)
    normed = held["nb"][at_rows, :].astype(F32)
    live = jnp.where(ins["count"][:1, :1] > slot.astype(F32), 1.0, 0.0)
    act_grad = jnp.dot(incoming.astype(BF16), ins["wut"][...], preferred_element_type=F32)
    pre_grad = (act_grad * gelu_pair(preact)[1]).astype(BF16).astype(F32)
    mean_one = jnp.sum(pre_grad * ins["wmean"][:1, :], axis=1, keepdims=True)
    mean_two = jnp.sum(pre_grad * preact, axis=1, keepdims=True) * (1.0 / width)
    norm_grad = jnp.dot(pre_grad.astype(BF16), ins["wdt"][...], preferred_element_type=F32)
    back = incoming + inv_std * (norm_grad - mean_one - normed * mean_two)
    if "send_b" in outs:
        outs["send_b"][...] = back.astype(BF16)
    rows = pl.ds(row, CHUNK)
    outs["dy"][rows, :] = (incoming * live).astype(BF16)
    outs["grads"][rows, :] = (back * live).astype(BF16)
    outs["pg"][rows, :] = (pre_grad * live).astype(BF16)


def turn_part(turn, ins, outs):
    width = ins["wd"].shape[0]
    part = pl.ds(turn * (width // TURNS), width // TURNS)
    outs["wdt"][:, part] = ins["wd"][part, :].T
    outs["wut"][part, :] = ins["wu"][:, part].T


def mean_part(ins, outs):
    total = jnp.sum(ins["wd"][...].astype(F32), axis=0, keepdims=True)
    outs["wmean"][...] = jnp.broadcast_to(total * (1.0 / ins["wd"].shape[0]), outs["wmean"].shape)
    count = ins["counts"][lax.axis_index("rep")].astype(F32)
    outs["count"][...] = jnp.full(outs["count"].shape, count)


class Loader:
    def __init__(self, ins, outs, sems, cuts):
        self.outs = outs
        self.copies = {}
        for at, (name, bounds) in enumerate(cuts.items()):
            source, target = ins["far_" + name], outs[name]
            self.copies[name] = [
                pltpu.make_async_copy(
                    source.at[begin:end], target.at[begin:end], sems.at[at, part]
                )
                for part, (begin, end) in enumerate(zip(bounds, bounds[1:]))
            ]
        for copies in self.copies.values():
            for copy in copies:
                copy.start()

    def wait(self, name, begin=0, end=None):
        for copy in self.copies[name][begin:end]:
            copy.wait()

    def __call__(self, name):
        self.wait(name)
        return self.outs[name][...]


def even_cuts(size):
    return [part * (size // PIECES) for part in range(PIECES + 1)]


def step_kernel(plan, names_in, names_out, *all_refs):
    step, sections, tokens, slot_rows, do_forward, do_backward, turn = plan
    ins = dict(zip(names_in, all_refs[: len(names_in)]))
    outs = dict(zip(names_out, all_refs[len(names_in) :]))
    section = lax.axis_index("section")
    chunks = tokens // CHUNK

    def place(at):
        inside = (at >= 0) & (at < chunks)
        clipped = jnp.clip(at, 0, chunks - 1) * CHUNK
        row = pl.multiple_of(jnp.where(inside, clipped, tokens), CHUNK)
        return row, pl.multiple_of(clipped, CHUNK)

    if do_backward:
        since = step - HOP * (sections - 1) - 1
        row, at_row = place(since - HOP * (sections - 1 - section))
        begin = min(since, chunks - 1) * CHUNK
        own = ins["g"][begin : begin + CHUNK, :]
        held = outs if do_forward else ins
        slot = at_row // slot_rows
        backward_part(row, at_row, own, section == sections - 1, slot, ins, held, outs)
    if do_forward:
        row, _ = place(step - HOP * section)
        begin = min(step, chunks - 1) * CHUNK
        if step == 0:
            cuts = {name: even_cuts(outs[name].shape[0]) for name in ("wd", "wu")}
            load = Loader(ins, outs, all_refs[-1], {"x": [0, CHUNK], **cuts})
            load.wait("x")
            forward_part(row, outs["x"][:CHUNK, :], section == 0, ins, outs, load)
        elif step == 1:
            middle = (2 * CHUNK + tokens) // 2
            load = Loader(ins, outs, all_refs[-1], {"x": [CHUNK, 2 * CHUNK, middle, tokens]})
            load.wait("x", 0, 1)
            own = outs["x"][CHUNK : 2 * CHUNK, :]
            forward_part(row, own, section == 0, ins, outs, lambda name: ins[name][...])
            load.wait("x", 1)
        else:
            own = ins["x"][begin : begin + CHUNK, :]
            forward_part(row, own, section == 0, ins, outs, lambda name: ins[name][...])
    if turn is not None and turn < TURNS:
        for part in range(TURNS):
            turn_part(part, ins, outs)
    if turn == TURNS:
        mean_part(ins, outs)


def run_step(plan, values, shapes, sends):
    step, sections, tokens, slot_rows, do_forward, do_backward, turn = plan
    names_in = []
    names_out = []
    if do_forward:
        first = [["far_x", "far_wd", "far_wu"], ["far_x", "recv_f", "wd", "wu"]]
        names_in += first[step] if step < 2 else ["x", "recv_f", "wd", "wu"]
        names_out += [["x", "wd", "wu"], ["x"]][step] if step < 2 else []
        names_out += ["send_f", "nb", "pre", "act", "std"]
    if do_backward:
        names_in += ["g", "recv_b", "wdt", "wut", "wmean", "count"]
        names_out += ["send_b", "dy", "grads", "pg"]
        if not do_forward:
            names_in += ["nb", "pre", "std"]
    if turn is not None and turn < TURNS:
        names_out += ["wdt", "wut"]
    if turn == TURNS:
        names_in += ["counts"]
        names_out += ["wmean", "count"]
    names_in = [k for k in names_in if not (k.startswith("recv") and k not in values)]
    names_out = [k for k in names_out if k in sends or not k.startswith("send")]
    aliases = {}
    for at, name in enumerate(names_out):
        if name in values and not name.startswith("send"):
            aliases[len(names_in)] = at
            names_in.append(name)

    def placed(name):
        if name in ("counts", "recv_f", "recv_b"):
            return values[name]
        return pltpu.with_memory_space_constraint(
            values[name], pltpu.HBM if name.startswith("far") else VM
        )

    def spec(name):
        if name.startswith("far"):
            return pl.BlockSpec(memory_space=pltpu.HBM)
        return pl.BlockSpec(memory_space=pltpu.SMEM if name == "counts" else VM)

    out_shape = [
        jax.ShapeDtypeStruct(*shapes[k]) if k.startswith("send") else VM(*shapes[k])
        for k in names_out
    ]
    width, bottleneck = shapes["wd"][0]
    results = pl.pallas_call(
        functools.partial(step_kernel, plan, names_in, names_out),
        out_shape=out_shape,
        in_specs=[spec(k) for k in names_in],
        out_specs=[pl.BlockSpec(memory_space=VM) for _ in names_out],
        input_output_aliases=aliases,
        scratch_shapes=[pltpu.SemaphoreType.DMA((3, PIECES))] if step < 2 else [],
        cost_estimate=pl.CostEstimate(
            flops=4 * CHUNK * width * bottleneck * (do_forward + do_backward),
            bytes_accessed=4 * width * bottleneck,
            transcendentals=CHUNK * bottleneck,
        ),
        compiler_params=pltpu.CompilerParams(vmem_limit_bytes=8 * 1024 * 1024),
        name="step_" + ("f" if do_forward else "") + ("b" if do_backward else ""),
    )(*[placed(k) for k in names_in])
    return dict(zip(names_out, results))


def outer(left, right):
    return lax.dot_general(left, right, (((0,), (0,)), ((), ())), preferred_element_type=F32)


def outer_down_kernel(tokens, reps, nb, pg, mine, other, held):
    core = lax.rem(lax.axis_index("rep"), 2)
    width = nb.shape[1]
    block = width // reps
    wide = 4 * block
    for at in range(width // wide):
        held[...] = outer(nb[:tokens, at * wide : (at + 1) * wide], pg[:tokens, :])
        for half in range(2):
            to = (2 * at + half) * block
            base = half * 2 * block
            mine[to : to + block, :] = held[pl.ds(base + core * block, block), :]
            other[to : to + block, :] = held[pl.ds(base + (1 - core) * block, block), :].astype(BF16)


def outer_up_kernel(tokens, reps, act, dy, mine, other, held, wide):
    core = lax.rem(lax.axis_index("rep"), 2)
    bottleneck, width = act.shape[1], dy.shape[1]
    chips = reps // 2
    rows = bottleneck // reps
    each = rows * (width // bottleneck)
    for at in range(width // bottleneck):
        held[...] = outer(act[:tokens, :], dy[:tokens, at * bottleneck : (at + 1) * bottleneck])
        for chip in range(chips):
            base = chip * 2 * rows
            to = chip * each + at * rows
            mine[to : to + rows, :] = held[pl.ds(base + core * rows, rows), :]
            wide[to : to + rows, :] = held[pl.ds(base + (1 - core) * rows, rows), :]
    other[...] = wide[...].astype(BF16)


def place_in(axis_first, side):
    chip = lax.axis_index("rep") // 2
    return chip // side if axis_first == "x" else lax.rem(chip, side)


def chip_sum_kernel(axis, side, mine, came, keep, *sends):
    me = place_in(axis, side)
    each = mine.shape[0] // (side * side)
    step, other = (side, 1) if axis == "x" else (1, side)
    for ahead, out in zip(DEALT, (keep, *sends)):
        to = lax.rem(me + ahead, side)
        for at in range(side):
            chip = to * step + at * other
            rows = pl.ds(pl.multiple_of(chip * each, each), each)
            part = mine[rows, :] + came[rows, :].astype(F32)
            out[at * each : (at + 1) * each, :] = part.astype(out.dtype)


def axis_sum_kernel(axis, side, keep, *refs):
    came, outs = refs[: side - 1], refs[side:]
    me = place_in("y" if axis == "x" else "x", side)
    each = keep.shape[0] // side
    for ahead, out in zip(DEALT, outs):
        to = lax.rem(me + ahead, side)
        rows = pl.ds(pl.multiple_of(to * each, each), each)
        total = keep[rows, :]
        for ref in came:
            total = total + ref[rows, :].astype(F32)
        out[...] = total.astype(out.dtype)


def final_kernel(side, counts, *refs):
    live = counts[0]
    for at in range(1, counts.shape[0]):
        live = live + counts[at]
    scale = live.astype(F32)
    for which, out in enumerate(refs[2 * side :]):
        total = refs[which * side][...]
        for ref in refs[which * side + 1 : (which + 1) * side]:
            total = total + ref[...].astype(F32)
        total = total / scale
        rows, bottleneck = out.shape[0], total.shape[1]
        for at in range(out.shape[1] // bottleneck):
            out[:, at * bottleneck : (at + 1) * bottleneck] = total[at * rows : (at + 1) * rows]


def store_kernel(tokens, grads, after, out, sems):
    size = tokens // COPIES
    copies = [
        pltpu.make_async_copy(
            grads.at[at * size : (at + 1) * size], out.at[at * size : (at + 1) * size], sems.at[at]
        )
        for at in range(COPIES)
    ]
    for copy in copies:
        copy.start()
    for copy in copies:
        copy.wait()


def call(kernel, name, out_shape, args, scratch=(), specs=None, out_specs=None):
    vmem = pl.BlockSpec(memory_space=VM)
    several = isinstance(out_shape, list)
    return pl.pallas_call(
        kernel,
        out_shape=out_shape,
        in_specs=specs or [vmem] * len(args),
        out_specs=out_specs or ([vmem] * len(out_shape) if several else vmem),
        scratch_shapes=list(scratch),
        compiler_params=pltpu.CompilerParams(vmem_limit_bytes=12 * 1024 * 1024),
        name=name,
    )(*args)


def weight_grads(values, tokens):
    reps = lax.axis_size("rep")
    chips = reps // 2
    side = round(chips**0.5)
    nb, act, dy, pg, grads = (
        pltpu.with_memory_space_constraint(values[k], VM) for k in ("nb", "act", "dy", "pg", "grads")
    )
    width, bottleneck = nb.shape[1], pg.shape[1]
    block = width // reps
    each = {"down": block, "up": (bottleneck // reps) * (width // bottleneck)}
    partner = [(i, i ^ 1) for i in range(reps)]

    def route(axis, ahead):
        def target(i):
            x, y, core = i // 2 // side, i // 2 % side, i % 2
            if axis == "x":
                x = (x + ahead) % side
            else:
                y = (y + ahead) % side
            return (x * side + y) * 2 + core

        return [(i, target(i)) for i in range(reps)]

    def outers(name, kernel, args, scratch):
        rows = chips * each[name]
        shapes = [VM((rows, bottleneck), F32), VM((rows, bottleneck), BF16)]
        mine, other = call(
            functools.partial(kernel, tokens, reps), "outer_" + name, shapes, args, scratch
        )
        return mine, lax.ppermute(other, "rep", partner)

    def parts(rows):
        sends = [jax.ShapeDtypeStruct((rows, bottleneck), BF16) for _ in range(side - 1)]
        return [VM((rows, bottleneck), F32), *sends]

    halves = {
        "down": outers("down", outer_down_kernel, (nb, pg), [VM((4 * block, bottleneck), F32)]),
        "up": outers(
            "up",
            outer_up_kernel,
            (act, dy),
            [VM((bottleneck, bottleneck), F32), VM((chips * each["up"], bottleneck), F32)],
        ),
    }
    first = {"down": "x", "up": "y"}
    second = {"down": "y", "up": "x"}
    sums, shares = {}, {}
    for name, (mine, came) in halves.items():
        mine = pltpu.with_memory_space_constraint(mine, VM)
        kernel = functools.partial(chip_sum_kernel, first[name], side)
        keep, *sends = call(kernel, "chip_sum_" + name, parts(side * each[name]), (mine, came))
        after = sends[-1]
        came = [lax.ppermute(s, "rep", route(first[name], k)) for k, s in zip(DEALT[1:], sends)]
        sums[name] = (keep, *came)
    any_spec = pl.BlockSpec(memory_space=pl.ANY)
    far_spec = pl.BlockSpec(memory_space=pltpu.HBM)
    grads_out = call(
        functools.partial(store_kernel, tokens),
        "store",
        pltpu.HBM((tokens, width), BF16),
        (grads, after),
        [pltpu.SemaphoreType.DMA((COPIES,))],
        [pl.BlockSpec(memory_space=VM), any_spec],
        far_spec,
    )
    stored = pltpu.with_memory_space_constraint(grads_out, pltpu.HBM)
    for name, (keep, *came) in sums.items():
        keep = pltpu.with_memory_space_constraint(keep, VM)
        kernel = functools.partial(axis_sum_kernel, first[name], side)
        args, specs = [keep, *came], [pl.BlockSpec(memory_space=VM)] * side
        keep, *sends = call(
            kernel, "axis_sum_" + name, parts(each[name]), [*args, stored], specs=[*specs, far_spec]
        )
        came = [lax.ppermute(s, "rep", route(second[name], k)) for k, s in zip(DEALT[1:], sends)]
        shares[name] = (keep, *came)
    args = [values["counts"]]
    for keep, *came in shares.values():
        args += [pltpu.with_memory_space_constraint(keep, VM), *came]
    shapes = [(block, bottleneck), (bottleneck // reps, width)]
    down, up = call(
        functools.partial(final_kernel, side),
        "final",
        [jax.ShapeDtypeStruct(shape, F32) for shape in shapes],
        args,
        specs=[pl.BlockSpec(memory_space=pltpu.SMEM)]
        + [pl.BlockSpec(memory_space=VM)] * (len(args) - 1),
    )
    return down, up, grads_out


def body(inputs, cotangent, w_down, w_up, counts):
    sections = lax.axis_size("section")
    slots, slot_rows, width = inputs.shape[1:]
    tokens = slots * slot_rows
    chunks = tokens // CHUNK
    bottleneck = w_down.shape[2]
    padded = tokens + CHUNK
    shapes = {
        "x": ((tokens, width), BF16),
        "wd": ((width, bottleneck), BF16),
        "wu": ((bottleneck, width), BF16),
        "wmean": ((8, bottleneck), F32),
        "count": ((8, 128), F32),
        "wdt": ((bottleneck, width), BF16),
        "wut": ((width, bottleneck), BF16),
        "send_f": ((CHUNK, width), BF16),
        "nb": ((padded, width), BF16),
        "pre": ((padded, bottleneck), F32),
        "act": ((padded, bottleneck), BF16),
        "std": ((padded, 128), F32),
        "send_b": ((CHUNK, width), BF16),
        "dy": ((padded, width), BF16),
        "grads": ((padded, width), BF16),
        "pg": ((padded, bottleneck), BF16),
    }
    values = {
        "counts": counts,
        "far_x": inputs.reshape(tokens, width),
        "far_wd": w_down[0],
        "far_wu": w_up[0],
        "g": cotangent.reshape(tokens, width),
    }
    ahead = [(i, (i + 1) % sections) for i in range(sections)]
    behind = [(b, a) for a, b in ahead]
    start = HOP * (sections - 1) + 1
    forward_steps = chunks + HOP * (sections - 1)
    ends = {"send_f": forward_steps, "send_b": start + forward_steps}
    moved = {"f": {}, "b": {}}
    for step in range(start + forward_steps):
        do_forward = step < forward_steps
        do_backward = step >= start
        turn = {2: 0, 4: TURNS}.get(step)
        for way in "fb":
            values.pop("recv_" + way, None)
            if step in moved[way]:
                values["recv_" + way] = moved[way].pop(step)
        plan = (step, sections, tokens, slot_rows, do_forward, do_backward, turn)
        sends = [k for k, end in ends.items() if step + HOP < end]
        results = run_step(plan, values, shapes, sends)
        for way, route in (("f", ahead), ("b", behind)):
            if "send_" + way in results:
                sent = results.pop("send_" + way)
                moved[way][step + HOP] = lax.ppermute(sent, "section", route)
        values.update(results)
    down_share, up_share, grads_out = weight_grads(values, tokens)
    return (
        down_share[None],
        up_share[None],
        grads_out.reshape(1, 1, slots, slot_rows, width),
    )


def solution(mesh):
    in_specs = (
        P("rep", None, None, None),
        P("rep", None, None, None),
        P("section", None, None),
        P("section", None, None),
        P(),
    )
    out_specs = (
        P("section", "rep", None),
        P("section", "rep", None),
        P("section", "rep", None, None, None),
    )
    return jax.shard_map(body, mesh=mesh, in_specs=in_specs, out_specs=out_specs, check_vma=False)
```
